32 devices in a mesh: dp: 2 (over core), ctx: 16 (over z, y, x).
Axes of the slice: x: 2, y: 2, z: 4, core: 2. Of those that a mesh axis runs over, the one named last changes fastest.
Arguments:
- doc_lengths: int32 [8], P('dp'), parts along dimension 0, may hold values from 1 to 1024, 2048 in all
- assignment: int32 [128], P('dp'), parts along dimension 0, may hold values from 0 to 63, each once
- queries: bfloat16 [4096, 4096], P(('dp', 'ctx')), parts along dimension 0, may hold values from -6 to 6
- key_state_rows: bfloat16 [4096, 512], P(('dp', 'ctx')), parts along dimension 0, may hold values from -6 to 6
- value_state_rows: bfloat16 [4096, 512], P(('dp', 'ctx')), parts along dimension 0, may hold values from -6 to 6
- out_grad: bfloat16 [4096, 4096], P(('dp', 'ctx')), parts along dimension 0, may hold values from -6 to 6
Outputs:
- attention_out: bfloat16 [4096, 4096], P(('dp', 'ctx')), parts along dimension 0
- query_grad: bfloat16 [4096, 4096], P(('dp', 'ctx')), parts along dimension 0
- key_gradient: bfloat16 [4096, 512], P(('dp', 'ctx')), parts along dimension 0
- value_gradient: bfloat16 [4096, 512], P(('dp', 'ctx')), parts along dimension 0
The draws below stay inside these ranges and needn't reach their ends.
There are 2 independent parts, one for each index of `dp`. The reference program is written for one: setup_inputs(seed, part) draws one part's arguments, and reference() takes and returns one part's arrays. A program takes and returns all parts, laid end to end along the dimension named above; each array names one. Nothing has to cross between parts.
Inputs may be any that keep to these rules, and one draw needn't show every extreme that they name: `assignment`: each of 0 to 63 once.
All inputs are finite; a program needn't handle non-finite values.
Results may differ from the reference program's by a relative error of at most 0.015.
Values may be sent and summed in bfloat16 or wider, within the bound.
A program may use at most 128 MiB of HBM per device.

```python
import math
import jax
import jax.numpy as jnp
import numpy as np
from jax import lax

DEVICE_TOKENS = 128
BLK = 32
MOST = 1024
QUERY_HEADS = 32
KEY_VALUE_HEADS = 4
HEAD_SIZE = 128
PACK_TOKENS = 2048
NBLK = 64
NDOC = 4
N_CTX = 16


def drawn_pair(key):
    base = jax.random.fold_in(key, 7)
    key_listing = jax.random.split(base, 4)
    query_draw = jnp.clip(jax.random.normal(key_listing[2], (PACK_TOKENS, QUERY_HEADS * HEAD_SIZE), jnp.float32), -6.0, 6.0)
    key_sample = jnp.clip(jax.random.normal(key_listing[3], (PACK_TOKENS, KEY_VALUE_HEADS * HEAD_SIZE), jnp.float32), -6.0, 6.0)
    return (query_draw, key_sample)


def draw_queries(key, part):
    return drawn_pair(key)[0].astype(jnp.bfloat16)


def draw_key_state_rows(key, part):
    return drawn_pair(key)[1].astype(jnp.bfloat16)


def steps_of(own_key, extent, shards, smallest, largest):
    level, own = 1.0, jax.random.fold_in(own_key, 6)
    for position, shards_of in shards:
        draws = jnp.exp(jax.random.uniform(jax.random.fold_in(own, position), (shards_of,), jnp.float32, smallest / len(shards), largest / len(shards)))
        level = level * jnp.repeat(draws, extent[position] // shards_of).reshape([-1 if axis == position else 1 for axis in range(len(extent))])
    return level


def split_up(amount, total, bound, lean):
    weights = [(1 << 20) // math.isqrt(standing ** lean) + 1 for standing in range(2, amount + 1)]
    surplus, given = total - bound - (amount - 1), [1] * (amount - 1)
    while surplus > 0:
        movable = [i for i in range(amount - 1) if given[i] < bound]
        whole, budget = sum([weights[i] for i in movable]), surplus
        for i in movable:
            more = min(bound - given[i], max(1, budget * weights[i] // whole), surplus)
            given[i] = given[i] + more
            surplus = surplus - more
    return np.array([bound] + given)


def uneven(rng, number_of, total, bound, lean):
    if number_of == 2:
        one = jax.random.randint(rng, (), max(1, total - bound), min(bound, total - 1) + 1)
        return jnp.stack([one, total - one])
    lengths = jnp.asarray(split_up(number_of, total, bound, lean), jnp.int32)
    couples = (number_of - 1) // 2
    source_of, receiver = lengths[1:1 + 2 * couples:2], lengths[2:2 + 2 * couples:2]
    margin = jnp.minimum(source_of - 1, bound - receiver)
    shifted = jax.random.randint(jax.random.fold_in(rng, 1), (couples,), 0, 1 << 20) % (margin + 1)
    lengths = lengths.at[1:1 + 2 * couples:2].set(source_of - shifted).at[2:2 + 2 * couples:2].set(receiver + shifted)
    return lengths[jax.random.permutation(jax.random.fold_in(rng, 2), number_of)]


def noise(stream_key, shape, scale, most, pieces=(), kind=jnp.bfloat16):
    entries = scale * jax.random.normal(stream_key, shape, jnp.float32)
    if pieces:
        entries = entries * steps_of(stream_key, shape, pieces, -0.22, 0.18)
    return jnp.clip(entries, -most, most).astype(kind)


def setup_inputs(seed: int = 0, part: int = 0) -> dict:
    seeds = jax.random.split(jax.random.key(seed), 7)
    own_keys = jax.random.split(jax.random.fold_in(seeds[6], part), 7)
    doc_lengths = uneven(own_keys[0], NDOC, PACK_TOKENS, MOST, 2).astype(jnp.int32)
    assignment = jax.random.permutation(own_keys[1], NBLK).astype(jnp.int32)
    queries = draw_queries(jax.random.fold_in(jax.random.fold_in(seeds[6], part), 71), part)
    key_state_rows = draw_key_state_rows(jax.random.fold_in(jax.random.fold_in(seeds[6], part), 71), part)
    value_state_rows = noise(own_keys[4], (PACK_TOKENS, KEY_VALUE_HEADS * HEAD_SIZE), 1.0, 6.0, ((0, 16),))
    out_grad = noise(own_keys[5], (PACK_TOKENS, QUERY_HEADS * HEAD_SIZE), 1.0, 6.0, ((0, 16),))
    return dict(doc_lengths=doc_lengths, assignment=assignment, queries=queries, key_state_rows=key_state_rows, value_state_rows=value_state_rows, out_grad=out_grad)


def rounded(values):
    return lax.optimization_barrier(values.astype(jnp.bfloat16)).astype(jnp.float32)


def places_of(assignment):
    slot_rows = jnp.arange(PACK_TOKENS, dtype=jnp.int32)
    return (assignment[slot_rows // BLK] * BLK + slot_rows % BLK).astype(jnp.int32)


def documents_of(doc_lengths, places):
    doc_bounds = jnp.cumsum(doc_lengths).astype(jnp.int32)
    return jnp.sum((doc_bounds[None, :] <= places[:, None]).astype(jnp.int32), axis=1)


def reference(doc_lengths, assignment, queries, key_state_rows, value_state_rows, out_grad):
    group_width = QUERY_HEADS // KEY_VALUE_HEADS
    score_scale = HEAD_SIZE ** -0.5
    key_places = places_of(assignment)
    doc_ids = documents_of(doc_lengths, key_places)
    key_complete = key_state_rows.reshape(PACK_TOKENS, KEY_VALUE_HEADS, HEAD_SIZE).astype(jnp.float32)
    value_complete = value_state_rows.reshape(PACK_TOKENS, KEY_VALUE_HEADS, HEAD_SIZE).astype(jnp.float32)

    def device_step(grand_totals, slices):
        query_piece, gradient_piece, query_place, query_doc = slices
        query_float = query_piece.reshape(DEVICE_TOKENS, KEY_VALUE_HEADS, group_width, HEAD_SIZE).astype(jnp.float32)
        gradient_float = gradient_piece.reshape(DEVICE_TOKENS, KEY_VALUE_HEADS, group_width, HEAD_SIZE).astype(jnp.float32)
        scores = jnp.einsum('qgjd,kgd->gjqk', query_float, key_complete) * score_scale
        allowed = (doc_ids[None, :] == query_doc[:, None]) & (key_places[None, :] <= query_place[:, None])
        masked = jnp.where(allowed, scores, -jnp.inf)
        row_top = jnp.max(masked, axis=-1, keepdims=True)
        log_total = row_top + jnp.log(jnp.sum(jnp.exp(masked - row_top), axis=-1, keepdims=True))
        attention = jnp.where(allowed, jnp.exp(scores - log_total), 0.0)
        attention_b = rounded(attention)
        output = jnp.einsum('gjqk,kgd->qgjd', attention_b, value_complete).astype(jnp.bfloat16)
        row_delta = jnp.sum(gradient_float * output.astype(jnp.float32), axis=-1)
        row_delta = jnp.transpose(row_delta, (1, 2, 0))[..., None]
        grad_weights = jnp.einsum('qgjd,kgd->gjqk', gradient_float, value_complete)
        dscore = rounded(attention * (grad_weights - row_delta) * score_scale)
        query_term = jnp.einsum('gjqk,kgd->qgjd', dscore, key_complete).astype(jnp.bfloat16)
        key_term = rounded(jnp.einsum('gjqk,qgjd->kgd', dscore, query_float))
        value_term = rounded(jnp.einsum('gjqk,qgjd->kgd', attention_b, gradient_float))
        grand_totals = (grand_totals[0] + key_term, grand_totals[1] + value_term)
        return grand_totals, (output.reshape(DEVICE_TOKENS, QUERY_HEADS * HEAD_SIZE), query_term.reshape(DEVICE_TOKENS, QUERY_HEADS * HEAD_SIZE))

    slices = (queries.reshape(N_CTX, DEVICE_TOKENS, QUERY_HEADS * HEAD_SIZE), out_grad.reshape(N_CTX, DEVICE_TOKENS, QUERY_HEADS * HEAD_SIZE),
              key_places.reshape(N_CTX, DEVICE_TOKENS), doc_ids.reshape(N_CTX, DEVICE_TOKENS))
    initial_sums = (jnp.zeros((PACK_TOKENS, KEY_VALUE_HEADS, HEAD_SIZE), jnp.float32), jnp.zeros((PACK_TOKENS, KEY_VALUE_HEADS, HEAD_SIZE), jnp.float32))
    grand_totals, stacked = lax.scan(device_step, initial_sums, slices)
    attention_out = stacked[0].reshape(PACK_TOKENS, QUERY_HEADS * HEAD_SIZE)
    query_grad = stacked[1].reshape(PACK_TOKENS, QUERY_HEADS * HEAD_SIZE)
    key_gradient = grand_totals[0].reshape(PACK_TOKENS, KEY_VALUE_HEADS * HEAD_SIZE).astype(jnp.bfloat16)
    value_gradient = grand_totals[1].reshape(PACK_TOKENS, KEY_VALUE_HEADS * HEAD_SIZE).astype(jnp.bfloat16)
    return attention_out, query_grad, key_gradient, value_gradient
```

```python
import functools

import jax
import jax.numpy as jnp
from jax import lax
from jax.experimental import pallas as pl
from jax.experimental.pallas import tpu as pltpu
from jax.sharding import PartitionSpec as P

BLK = 32
HEAD = 128
LOG2E = 1.4426950408889634
F32 = jnp.float32
BF16 = jnp.bfloat16


def nt(a, b):
    return lax.dot_general(a, b, (((1,), (1,)), ((), ())), preferred_element_type=F32)


def nn(a, b):
    return jnp.dot(a, b, preferred_element_type=F32)


def kernel(
    planes, groups, pairs,
    bias_ref, q_ref, k_ref, v_ref, do_ref,
    out_ref, dq_ref, dk_ref, dv_ref,
    kvb, part, half, zbuf, lastb, s_buf, e_buf, kt, vt, acc,
    ag_send, ag_recv, rs_send, rs_recv,
):
    rows = q_ref.shape[0]
    tile = 4 * rows
    scale = HEAD ** (-0.5)
    me = lax.axis_index("ctx")
    x = lax.rem(me, 2)
    y = lax.rem(me // 2, 2)
    z = me // 4
    peer_x = me + 1 - 2 * x
    peer_y = me + 2 - 4 * y
    top = planes - 1

    def remote(src, dst, send, recv, device):
        return pltpu.make_async_remote_copy(
            src_ref=src, dst_ref=dst, send_sem=send, recv_sem=recv,
            device_id={"ctx": device}, device_id_type=pl.DeviceIdType.MESH,
        )

    def ag_copy(g, v, index, ref, device):
        return remote(ref, ref, ag_send.at[g, v, index], ag_recv.at[g, v, index], device)

    def pair_of(g, v, plane):
        return kvb.at[g, 0, plane, y] if v == 0 else kvb.at[g, 1, plane, :, x]

    def ag_first(g, v):
        return ag_copy(g, v, 0, kvb.at[g, v, z, y, x], peer_x if v == 0 else peer_y)

    def ag_first_in(g, v):
        ref = kvb.at[g, 0, z, y, 1 - x] if v == 0 else kvb.at[g, 1, z, 1 - y, x]
        return ag_copy(g, v, 0, ref, peer_x if v == 0 else peer_y)

    def ag_up(g, v, j, plane):
        return ag_copy(g, v, 1 + j, pair_of(g, v, plane), me + 4)

    def ag_down(g, v, j, plane):
        return ag_copy(g, v, planes + j, pair_of(g, v, plane), me - 4)

    def ag_last(g, v, plane):
        return ag_copy(g, v, 2 * planes - 1 + plane, pair_of(g, v, plane), peer_y if v == 0 else peer_x)

    def ag_last_in(g, v, plane):
        ref = kvb.at[g, 0, plane, 1 - y] if v == 0 else kvb.at[g, 1, plane, :, 1 - x]
        return ag_copy(g, v, 2 * planes - 1 + plane, ref, peer_y if v == 0 else peer_x)

    def ag_step(k, g):
        for v in range(2):
            if k == 0:
                ag_first(g, v).start()
            elif k == 1:
                ag_first_in(g, v).wait_recv()

                @pl.when(z < top)
                def _():
                    ag_up(g, v, 0, z).start()

                @pl.when(z > 0)
                def _():
                    ag_down(g, v, 0, z).start()

                ag_last(g, v, z).start()
            elif k <= planes:
                j = k - 1

                @pl.when(z >= j)
                def _():
                    ag_up(g, v, j - 1, z - j).wait_recv()
                    if j < top:
                        @pl.when(z < top)
                        def _():
                            ag_up(g, v, j, z - j).start()
                    ag_last(g, v, z - j).start()

                @pl.when(z + j <= top)
                def _():
                    ag_down(g, v, j - 1, z + j).wait_recv()
                    if j < top:
                        @pl.when(z > 0)
                        def _():
                            ag_down(g, v, j, z + j).start()
                    ag_last(g, v, z + j).start()
            else:
                for plane in range(planes):
                    ag_last_in(g, v, plane).wait_recv()
                    ag_last(g, v, plane).wait_send()
                ag_first(g, v).wait_send()
                for j in range(top):
                    @pl.when(jnp.logical_and(z < top, z >= j))
                    def _():
                        ag_up(g, v, j, z - j).wait_send()

                    @pl.when(jnp.logical_and(z > 0, z + j <= top))
                    def _():
                        ag_down(g, v, j, z + j).wait_send()

    def rs_half(g, v):
        src = part.at[g, 0, :, 1 - y] if v == 0 else part.at[g, 1, :, :, 1 - x]
        return remote(src, half.at[g, v], rs_send.at[g, v, 0], rs_recv.at[g, v, 0],
                      peer_y if v == 0 else peer_x)

    def rs_flow(g, v, way, t):
        index = 1 + way * planes + t
        return remote(half.at[g, v, t], zbuf.at[g, v, way, t], rs_send.at[g, v, index],
                      rs_recv.at[g, v, index], me + 4 - 8 * way)

    def rs_last(g, v):
        index = 1 + 2 * planes
        src = half.at[g, 0, z, 1 - x] if v == 0 else half.at[g, 1, z, 1 - y]
        return remote(src, lastb.at[g, v], rs_send.at[g, v, index], rs_recv.at[g, v, index],
                      peer_x if v == 0 else peer_y)

    def rs_step(k, g):
        for v in range(2):
            if k == 0:
                rs_half(g, v).start()
                continue
            if k == 1:
                rs_half(g, v).wait_recv()
                own = part[g, 0, :, y] if v == 0 else part[g, 1, :, :, x]
                half[g, v] = (half[g, v].astype(F32) + own.astype(F32)).astype(BF16)
            if k <= planes:
                s = k - 1
                for way in range(2):
                    place = z if way == 0 else top - z
                    dist = top - (s - place)
                    t = dist if way == 0 else top - dist

                    @pl.when(jnp.logical_and(s >= place, dist >= place))
                    def _():
                        @pl.when(place > 0)
                        def _():
                            rs_flow(g, v, way, t).wait_recv()
                            half[g, v, t] = (
                                half[g, v, t].astype(F32) + zbuf[g, v, way, t].astype(F32)
                            ).astype(BF16)

                        @pl.when(dist > place)
                        def _():
                            rs_flow(g, v, way, t).start()
            if k == planes:
                rs_last(g, v).start()
            if k == planes + 1:
                rs_last(g, v).wait_recv()
                own = half[g, 0, z, x] if v == 0 else half[g, 1, z, y]
                total = (own.astype(F32) + lastb[g, v].astype(F32)).astype(BF16)
                cols = pl.ds(pl.multiple_of(g * HEAD, HEAD), HEAD)
                (dk_ref if v == 0 else dv_ref)[:, cols] = total
                rs_half(g, v).wait_send()
                rs_last(g, v).wait_send()
                for t in range(planes):
                    @pl.when(t > z)
                    def _():
                        rs_flow(g, v, 0, t).wait_send()

                    @pl.when(t < z)
                    def _():
                        rs_flow(g, v, 1, t).wait_send()

    steps = planes + 2

    barrier = pltpu.get_barrier_semaphore()
    for peer in (peer_x, peer_y):
        pl.semaphore_signal(barrier, inc=1, device_id={"ctx": peer}, device_id_type=pl.DeviceIdType.MESH)

    @pl.when(z < top)
    def _():
        pl.semaphore_signal(barrier, inc=1, device_id={"ctx": me + 4}, device_id_type=pl.DeviceIdType.MESH)

    @pl.when(z > 0)
    def _():
        pl.semaphore_signal(barrier, inc=1, device_id={"ctx": me - 4}, device_id_type=pl.DeviceIdType.MESH)

    for g in range(groups):
        kvb[g, 0, z, y, x] = k_ref[:, g * HEAD:(g + 1) * HEAD]
        kvb[g, 1, z, y, x] = v_ref[:, g * HEAD:(g + 1) * HEAD]
    pl.semaphore_wait(barrier, 2 + (z < top).astype(jnp.int32) + (z > 0).astype(jnp.int32))

    for g in range(groups):
        ag_step(0, g)
    for k in range(1, steps):
        ag_step(k, 0)

    points = 2 * pairs

    def beside(place, g, p):
        for k in range(steps):
            point = min(k, points - 1)
            if point % 2 != place:
                continue

            @pl.when(p == point // 2)
            def _():
                if k > 0:
                    @pl.when(g < groups - 1)
                    def _():
                        ag_step(k, g + 1)

                @pl.when(g > 0)
                def _():
                    rs_step(k, g - 1)

    def keys(g, v, t):
        return kvb[g, v, t].reshape(tile, HEAD)

    def head(g, carry):
        for t in range(planes):
            kt[:, t * tile:(t + 1) * tile] = keys(g, 0, t).T
            vt[:, t * tile:(t + 1) * tile] = keys(g, 1, t).T
        acc[...] = jnp.zeros_like(acc)

        def pair(p, carry):
            start = pl.multiple_of((g * pairs + p) * 2 * HEAD, HEAD)
            col0 = pl.ds(start, HEAD)
            col1 = pl.ds(pl.multiple_of(start + HEAD, HEAD), HEAD)
            q2 = jnp.concatenate([q_ref[:, col0], q_ref[:, col1]], axis=0)
            wide = q2.shape[0]
            most = jnp.full((8, wide), -jnp.inf, F32)
            for t in range(planes):
                b = bias_ref[t * tile:(t + 1) * tile, :]
                s = nt(keys(g, 0, t), q2) + jnp.concatenate([b, b], axis=1)
                s_buf[t * tile:(t + 1) * tile, :] = s
                most = jnp.maximum(most, jnp.max(s.reshape(tile // 8, 8, wide), axis=0))
            beside(0, g, p)
            lift = jnp.max(most, axis=0, keepdims=True) * (scale * LOG2E)
            total = jnp.zeros((8, wide), F32)
            o_t = jnp.zeros((HEAD, wide), F32)
            for t in range(planes):
                e = jnp.exp2(s_buf[t * tile:(t + 1) * tile, :] * (scale * LOG2E) - lift)
                total = total + jnp.sum(e.reshape(tile // 8, 8, wide), axis=0)
                eb = e.astype(BF16)
                e_buf[t * tile:(t + 1) * tile, :] = eb
                o_t = o_t + nn(vt[:, t * tile:(t + 1) * tile], eb)
            inv = 1.0 / jnp.sum(total, axis=0, keepdims=True)
            o_t = (o_t * inv).astype(BF16).astype(F32)
            o2 = o_t.T.astype(BF16)
            out_ref[:, col0] = o2[:rows]
            out_ref[:, col1] = o2[rows:]
            do2 = jnp.concatenate([do_ref[:, col0], do_ref[:, col1]], axis=0).astype(F32)
            delta = jnp.sum(do2.T * o_t, axis=0, keepdims=True) * inv
            dos = (do2 * jnp.broadcast_to(inv, (HEAD, wide)).T).astype(BF16)
            dq_t = jnp.zeros((HEAD, wide), F32)
            for t in range(planes):
                span = slice(t * tile, (t + 1) * tile)
                dp = nt(keys(g, 1, t), dos)
                eb = e_buf[span, :]
                ds = (eb.astype(F32) * (dp - delta)).astype(BF16)
                acc[0, span, :] += nn(ds, q2)
                acc[1, span, :] += nn(eb, dos)
                dq_t = dq_t + nn(kt[:, span], ds)
            dq2 = (dq_t * scale).T.astype(BF16)
            dq_ref[:, col0] = dq2[:rows]
            dq_ref[:, col1] = dq2[rows:]
            beside(1, g, p)
            return carry

        lax.fori_loop(0, pairs, pair, 0)
        for t in range(planes):
            span = slice(t * tile, (t + 1) * tile)
            part[g, 0, t] = (acc[0, span, :] * scale).astype(BF16).reshape(2, 2, rows, HEAD)
            part[g, 1, t] = acc[1, span, :].astype(BF16).reshape(2, 2, rows, HEAD)
        return carry

    lax.fori_loop(0, groups, head, 0)
    for k in range(steps):
        rs_step(k, groups - 1)


def body(doc_lengths, assignment, queries, key_state_rows, value_state_rows, out_grad):
    rows = queries.shape[0]
    blocks = assignment.shape[0]
    total = blocks * BLK
    devices = total // rows
    planes = devices // 4
    groups = key_state_rows.shape[1] // HEAD
    pairs = queries.shape[1] // key_state_rows.shape[1] // 2
    bounds = jnp.cumsum(doc_lengths)
    per = rows // BLK
    own = lax.dynamic_slice_in_dim(assignment, lax.axis_index("ctx") * per, per)
    offset = jnp.arange(BLK, dtype=jnp.int32)
    key_place = (assignment[:, None] * BLK + offset[None, :]).reshape(-1)
    query_place = (own[:, None] * BLK + offset[None, :]).reshape(-1)
    key_doc = jnp.sum((bounds[None, :] <= key_place[:, None]).astype(jnp.int32), axis=1)
    query_doc = jnp.sum((bounds[None, :] <= query_place[:, None]).astype(jnp.int32), axis=1)
    allowed = (key_doc[:, None] == query_doc[None, :]) & (key_place[:, None] <= query_place[None, :])
    bias = jnp.where(allowed, 0.0, -1e30).astype(F32)

    ag_sems = 3 * planes - 1
    rs_sems = 2 * planes + 2
    vmem = pl.BlockSpec(memory_space=pltpu.VMEM)
    return pl.pallas_call(
        functools.partial(kernel, planes, groups, pairs),
        out_shape=(
            jax.ShapeDtypeStruct(queries.shape, BF16),
            jax.ShapeDtypeStruct(queries.shape, BF16),
            jax.ShapeDtypeStruct(key_state_rows.shape, BF16),
            jax.ShapeDtypeStruct(key_state_rows.shape, BF16),
        ),
        in_specs=[vmem] * 5,
        out_specs=(vmem,) * 4,
        scratch_shapes=[
            pltpu.VMEM((groups, 2, planes, 2, 2, rows, HEAD), BF16),
            pltpu.VMEM((groups, 2, planes, 2, 2, rows, HEAD), BF16),
            pltpu.VMEM((groups, 2, planes, 2, rows, HEAD), BF16),
            pltpu.VMEM((groups, 2, 2, planes, 2, rows, HEAD), BF16),
            pltpu.VMEM((groups, 2, rows, HEAD), BF16),
            pltpu.VMEM((total, 2 * rows), F32),
            pltpu.VMEM((total, 2 * rows), BF16),
            pltpu.VMEM((HEAD, total), BF16),
            pltpu.VMEM((HEAD, total), BF16),
            pltpu.VMEM((2, total, HEAD), F32),
            pltpu.SemaphoreType.DMA((groups, 2, ag_sems)),
            pltpu.SemaphoreType.DMA((groups, 2, ag_sems)),
            pltpu.SemaphoreType.DMA((groups, 2, rs_sems)),
            pltpu.SemaphoreType.DMA((groups, 2, rs_sems)),
        ],
        compiler_params=pltpu.CompilerParams(
            collective_id=0, has_side_effects=True, vmem_limit_bytes=58 * 1024 * 1024
        ),
        cost_estimate=pl.CostEstimate(
            flops=12 * queries.shape[0] * queries.shape[1] * total,
            bytes_accessed=8 * queries.size,
            transcendentals=queries.shape[0] * queries.shape[1] // HEAD * total,
        ),
    )(bias, queries, key_state_rows, value_state_rows, out_grad)


def solution(mesh):
    row = P(("dp", "ctx"), None)
    return jax.shard_map(
        body,
        mesh=mesh,
        in_specs=(P("dp"), P("dp"), row, row, row, row),
        out_specs=(row, row, row, row),
        check_vma=False,
    )
```

```python
import functools

import jax
import jax.numpy as jnp
from jax import lax
from jax.experimental import pallas as pl
from jax.experimental.pallas import tpu as pltpu
from jax.sharding import PartitionSpec as P

BLK = 32
HEAD = 128
LOG2E = 1.4426950408889634
F32 = jnp.float32
BF16 = jnp.bfloat16


def nt(a, b):
    return lax.dot_general(a, b, (((1,), (1,)), ((), ())), preferred_element_type=F32)


def nn(a, b):
    return jnp.dot(a, b, preferred_element_type=F32)


def kernel(
    planes, groups, pairs,
    bias_ref, q_ref, k_ref, v_ref, do_ref,
    out_ref, dq_ref, dk_ref, dv_ref,
    kvb, part, half, zbuf, lastb, s_buf, e_buf, kt, vt, acc, sums,
    ag_send, ag_recv, rs_send, rs_recv,
):
    rows = q_ref.shape[0]
    tile = 4 * rows
    scale = HEAD ** (-0.5)
    me = lax.axis_index("ctx")
    x = lax.rem(me, 2)
    y = lax.rem(me // 2, 2)
    z = me // 4
    peer_x = me + 1 - 2 * x
    peer_y = me + 2 - 4 * y
    top = planes - 1

    def remote(src, dst, send, recv, device):
        return pltpu.make_async_remote_copy(
            src_ref=src, dst_ref=dst, send_sem=send, recv_sem=recv,
            device_id={"ctx": device}, device_id_type=pl.DeviceIdType.MESH,
        )

    def ag_copy(g, v, index, ref, device):
        return remote(ref, ref, ag_send.at[g, v, index], ag_recv.at[g, v, index], device)

    def pair_of(g, v, plane):
        return kvb.at[g, 0, plane, y] if v == 0 else kvb.at[g, 1, plane, :, x]

    def ag_first(g, v):
        return ag_copy(g, v, 0, kvb.at[g, v, z, y, x], peer_x if v == 0 else peer_y)

    def ag_first_in(g, v):
        ref = kvb.at[g, 0, z, y, 1 - x] if v == 0 else kvb.at[g, 1, z, 1 - y, x]
        return ag_copy(g, v, 0, ref, peer_x if v == 0 else peer_y)

    def ag_up(g, v, j, plane):
        return ag_copy(g, v, 1 + j, pair_of(g, v, plane), me + 4)

    def ag_down(g, v, j, plane):
        return ag_copy(g, v, planes + j, pair_of(g, v, plane), me - 4)

    def ag_last(g, v, plane):
        return ag_copy(g, v, 2 * planes - 1 + plane, pair_of(g, v, plane), peer_y if v == 0 else peer_x)

    def ag_last_in(g, v, plane):
        ref = kvb.at[g, 0, plane, 1 - y] if v == 0 else kvb.at[g, 1, plane, :, 1 - x]
        return ag_copy(g, v, 2 * planes - 1 + plane, ref, peer_y if v == 0 else peer_x)

    def ag_step(k, g):
        for v in range(2):
            if k == 0:
                ag_first(g, v).start()
            elif k == 1:
                ag_first_in(g, v).wait_recv()

                @pl.when(z < top)
                def _():
                    ag_up(g, v, 0, z).start()

                @pl.when(z > 0)
                def _():
                    ag_down(g, v, 0, z).start()

                ag_last(g, v, z).start()
            elif k <= planes:
                j = k - 1

                @pl.when(z >= j)
                def _():
                    ag_up(g, v, j - 1, z - j).wait_recv()
                    if j < top:
                        @pl.when(z < top)
                        def _():
                            ag_up(g, v, j, z - j).start()
                    ag_last(g, v, z - j).start()

                @pl.when(z + j <= top)
                def _():
                    ag_down(g, v, j - 1, z + j).wait_recv()
                    if j < top:
                        @pl.when(z > 0)
                        def _():
                            ag_down(g, v, j, z + j).start()
                    ag_last(g, v, z + j).start()
            else:
                for plane in range(planes):
                    ag_last_in(g, v, plane).wait_recv()
                    ag_last(g, v, plane).wait_send()
                ag_first(g, v).wait_send()
                for j in range(top):
                    @pl.when(jnp.logical_and(z < top, z >= j))
                    def _():
                        ag_up(g, v, j, z - j).wait_send()

                    @pl.when(jnp.logical_and(z > 0, z + j <= top))
                    def _():
                        ag_down(g, v, j, z + j).wait_send()

    def rs_half(g, v, t):
        src = part.at[g, 0, t, 1 - y] if v == 0 else part.at[g, 1, t, :, 1 - x]
        index = 2 * planes + 1 + t
        return remote(src, half.at[g, v, t], rs_send.at[g, v, index], rs_recv.at[g, v, index],
                      peer_y if v == 0 else peer_x)

    def rs_flow(g, v, way, t):
        index = way * planes + t
        return remote(half.at[g, v, t], zbuf.at[g, v, way, t], rs_send.at[g, v, index],
                      rs_recv.at[g, v, index], me + 4 - 8 * way)

    def rs_last(g, v):
        index = 2 * planes
        src = half.at[g, 0, z, 1 - x] if v == 0 else half.at[g, 1, z, 1 - y]
        return remote(src, lastb.at[g, v], rs_send.at[g, v, index], rs_recv.at[g, v, index],
                      peer_x if v == 0 else peer_y)

    def joined(g, v, t):
        own = part[g, 0, t, y] if v == 0 else part[g, 1, t, :, x]
        return half[g, v, t].astype(F32) + own.astype(F32)

    def rs_step(k, g):
        if k == 0:
            for i in range(planes):
                for v in range(2):
                    @pl.when(top - i > z)
                    def _():
                        rs_half(g, v, top - i).start()

                    @pl.when(i < z)
                    def _():
                        rs_half(g, v, i).start()
            for v in range(2):
                rs_half(g, v, z).start()
            return
        for v in range(2):
            if k < planes:
                s = k - 1
                for way in range(2):
                    place = z if way == 0 else top - z
                    dist = top - (s - place)
                    t = dist if way == 0 else top - dist

                    @pl.when(jnp.logical_and(s >= place, dist > place))
                    def _():
                        rs_half(g, v, t).wait_recv()

                        @pl.when(place == 0)
                        def _():
                            half[g, v, t] = joined(g, v, t).astype(BF16)

                        @pl.when(place > 0)
                        def _():
                            rs_flow(g, v, way, t).wait_recv()
                            half[g, v, t] = (joined(g, v, t) + zbuf[g, v, way, t].astype(F32)).astype(BF16)

                        rs_flow(g, v, way, t).start()
            elif k == planes:
                rs_half(g, v, z).wait_recv()
                sums[...] = joined(g, v, z)

                @pl.when(z > 0)
                def _():
                    rs_flow(g, v, 0, z).wait_recv()
                    sums[...] += zbuf[g, v, 0, z].astype(F32)

                @pl.when(z < top)
                def _():
                    rs_flow(g, v, 1, z).wait_recv()
                    sums[...] += zbuf[g, v, 1, z].astype(F32)

                half[g, v, z] = sums[...].astype(BF16)
                rs_last(g, v).start()
            else:
                rs_last(g, v).wait_recv()
                own = half[g, 0, z, x] if v == 0 else half[g, 1, z, y]
                total = (own.astype(F32) + lastb[g, v].astype(F32)).astype(BF16)
                cols = pl.ds(pl.multiple_of(g * HEAD, HEAD), HEAD)
                (dk_ref if v == 0 else dv_ref)[:, cols] = total
                rs_last(g, v).wait_send()
                for t in range(planes):
                    rs_half(g, v, t).wait_send()

                    @pl.when(t > z)
                    def _():
                        rs_flow(g, v, 0, t).wait_send()

                    @pl.when(t < z)
                    def _():
                        rs_flow(g, v, 1, t).wait_send()

    steps = planes + 2

    barrier = pltpu.get_barrier_semaphore()
    for peer in (peer_x, peer_y):
        pl.semaphore_signal(barrier, inc=1, device_id={"ctx": peer}, device_id_type=pl.DeviceIdType.MESH)

    @pl.when(z < top)
    def _():
        pl.semaphore_signal(barrier, inc=1, device_id={"ctx": me + 4}, device_id_type=pl.DeviceIdType.MESH)

    @pl.when(z > 0)
    def _():
        pl.semaphore_signal(barrier, inc=1, device_id={"ctx": me - 4}, device_id_type=pl.DeviceIdType.MESH)

    for g in range(groups):
        kvb[g, 0, z, y, x] = k_ref[:, g * HEAD:(g + 1) * HEAD]
        kvb[g, 1, z, y, x] = v_ref[:, g * HEAD:(g + 1) * HEAD]
    pl.semaphore_wait(barrier, 2 + (z < top).astype(jnp.int32) + (z > 0).astype(jnp.int32))

    def ag_slot(slot):
        for g in reversed(range(groups)):
            if slot == 2 * g:
                ag_step(0, g)
        for g in range(groups):
            if 0 < slot - 2 * g < steps:
                ag_step(slot - 2 * g, g)

    for slot in range(steps):
        ag_slot(slot)

    points = 2 * pairs

    def beside(place, g, p):
        here = g * points + 2 * p + place
        for i in range(2 * (groups - 1)):
            if (1 + 2 * i) % 2 == place:
                @pl.when(here == 1 + 2 * i)
                def _():
                    ag_slot(steps + i)
        for k in range(steps):
            point = min(k if k == 0 else k + 1, points - 1)
            if point % 2 == place:
                @pl.when(jnp.logical_and(p == point // 2, g > 0))
                def _():
                    rs_step(k, g - 1)

    def keys(g, v, t):
        return kvb[g, v, t].reshape(tile, HEAD)

    def head(g, carry):
        for t in range(planes):
            kt[:, t * tile:(t + 1) * tile] = keys(g, 0, t).T
            vt[:, t * tile:(t + 1) * tile] = keys(g, 1, t).T
        acc[...] = jnp.zeros_like(acc)

        def pair(p, carry):
            start = pl.multiple_of((g * pairs + p) * 2 * HEAD, HEAD)
            col0 = pl.ds(start, HEAD)
            col1 = pl.ds(pl.multiple_of(start + HEAD, HEAD), HEAD)
            q2 = jnp.concatenate([q_ref[:, col0], q_ref[:, col1]], axis=0)
            wide = q2.shape[0]
            most = jnp.full((8, wide), -jnp.inf, F32)
            for t in range(planes):
                b = bias_ref[t * tile:(t + 1) * tile, :]
                s = nt(keys(g, 0, t), q2) + jnp.concatenate([b, b], axis=1)
                s_buf[t * tile:(t + 1) * tile, :] = s
                most = jnp.maximum(most, jnp.max(s.reshape(tile // 8, 8, wide), axis=0))
            beside(0, g, p)
            lift = jnp.max(most, axis=0, keepdims=True) * (scale * LOG2E)
            total = jnp.zeros((8, wide), F32)
            o_t = jnp.zeros((HEAD, wide), F32)
            for t in range(planes):
                e = jnp.exp2(s_buf[t * tile:(t + 1) * tile, :] * (scale * LOG2E) - lift)
                total = total + jnp.sum(e.reshape(tile // 8, 8, wide), axis=0)
                eb = e.astype(BF16)
                e_buf[t * tile:(t + 1) * tile, :] = eb
                o_t = o_t + nn(vt[:, t * tile:(t + 1) * tile], eb)
            inv = 1.0 / jnp.sum(total, axis=0, keepdims=True)
            o_t = (o_t * inv).astype(BF16).astype(F32)
            o2 = o_t.T.astype(BF16)
            out_ref[:, col0] = o2[:rows]
            out_ref[:, col1] = o2[rows:]
            do2 = jnp.concatenate([do_ref[:, col0], do_ref[:, col1]], axis=0).astype(F32)
            delta = jnp.sum(do2.T * o_t, axis=0, keepdims=True) * inv
            dos = (do2 * jnp.broadcast_to(inv, (HEAD, wide)).T).astype(BF16)
            dq_t = jnp.zeros((HEAD, wide), F32)
            for t in range(planes):
                span = slice(t * tile, (t + 1) * tile)
                dp = nt(keys(g, 1, t), dos)
                eb = e_buf[span, :]
                ds = (eb.astype(F32) * (dp - delta)).astype(BF16)
                acc[0, span, :] += nn(ds, q2)
                acc[1, span, :] += nn(eb, dos)
                dq_t = dq_t + nn(kt[:, span], ds)
            dq2 = (dq_t * scale).T.astype(BF16)
            dq_ref[:, col0] = dq2[:rows]
            dq_ref[:, col1] = dq2[rows:]
            beside(1, g, p)
            return carry

        lax.fori_loop(0, pairs, pair, 0)
        for t in range(planes):
            span = slice(t * tile, (t + 1) * tile)
            part[g, 0, t] = (acc[0, span, :] * scale).astype(BF16).reshape(2, 2, rows, HEAD)
            part[g, 1, t] = acc[1, span, :].astype(BF16).reshape(2, 2, rows, HEAD)
        return carry

    lax.fori_loop(0, groups, head, 0)
    for k in range(steps):
        rs_step(k, groups - 1)


def body(doc_lengths, assignment, queries, key_state_rows, value_state_rows, out_grad):
    rows = queries.shape[0]
    blocks = assignment.shape[0]
    total = blocks * BLK
    devices = total // rows
    planes = devices // 4
    groups = key_state_rows.shape[1] // HEAD
    pairs = queries.shape[1] // key_state_rows.shape[1] // 2
    bounds = jnp.cumsum(doc_lengths)
    per = rows // BLK
    own = lax.dynamic_slice_in_dim(assignment, lax.axis_index("ctx") * per, per)
    offset = jnp.arange(BLK, dtype=jnp.int32)
    key_place = (assignment[:, None] * BLK + offset[None, :]).reshape(-1)
    query_place = (own[:, None] * BLK + offset[None, :]).reshape(-1)
    key_doc = jnp.sum((bounds[None, :] <= key_place[:, None]).astype(jnp.int32), axis=1)
    query_doc = jnp.sum((bounds[None, :] <= query_place[:, None]).astype(jnp.int32), axis=1)
    allowed = (key_doc[:, None] == query_doc[None, :]) & (key_place[:, None] <= query_place[None, :])
    bias = jnp.where(allowed, 0.0, -1e30).astype(F32)

    ag_sems = 3 * planes - 1
    rs_sems = 3 * planes + 1
    vmem = pl.BlockSpec(memory_space=pltpu.VMEM)
    return pl.pallas_call(
        functools.partial(kernel, planes, groups, pairs),
        out_shape=(
            jax.ShapeDtypeStruct(queries.shape, BF16),
            jax.ShapeDtypeStruct(queries.shape, BF16),
            jax.ShapeDtypeStruct(key_state_rows.shape, BF16),
            jax.ShapeDtypeStruct(key_state_rows.shape, BF16),
        ),
        in_specs=[vmem] * 5,
        out_specs=(vmem,) * 4,
        scratch_shapes=[
            pltpu.VMEM((groups, 2, planes, 2, 2, rows, HEAD), BF16),
            pltpu.VMEM((groups, 2, planes, 2, 2, rows, HEAD), BF16),
            pltpu.VMEM((groups, 2, planes, 2, rows, HEAD), BF16),
            pltpu.VMEM((groups, 2, 2, planes, 2, rows, HEAD), BF16),
            pltpu.VMEM((groups, 2, rows, HEAD), BF16),
            pltpu.VMEM((total, 2 * rows), F32),
            pltpu.VMEM((total, 2 * rows), BF16),
            pltpu.VMEM((HEAD, total), BF16),
            pltpu.VMEM((HEAD, total), BF16),
            pltpu.VMEM((2, total, HEAD), F32),
            pltpu.VMEM((2, rows, HEAD), F32),
            pltpu.SemaphoreType.DMA((groups, 2, ag_sems)),
            pltpu.SemaphoreType.DMA((groups, 2, ag_sems)),
            pltpu.SemaphoreType.DMA((groups, 2, rs_sems)),
            pltpu.SemaphoreType.DMA((groups, 2, rs_sems)),
        ],
        compiler_params=pltpu.CompilerParams(
            collective_id=0, has_side_effects=True, vmem_limit_bytes=58 * 1024 * 1024
        ),
        cost_estimate=pl.CostEstimate(
            flops=12 * queries.shape[0] * queries.shape[1] * total,
            bytes_accessed=8 * queries.size,
            transcendentals=queries.shape[0] * queries.shape[1] // HEAD * total,
        ),
    )(bias, queries, key_state_rows, value_state_rows, out_grad)


def solution(mesh):
    row = P(("dp", "ctx"), None)
    return jax.shard_map(
        body,
        mesh=mesh,
        in_specs=(P("dp"), P("dp"), row, row, row, row),
        out_specs=(row, row, row, row),
        check_vma=False,
    )
```

```python
import functools

import jax
import jax.numpy as jnp
from jax import lax
from jax.experimental import pallas as pl
from jax.experimental.pallas import tpu as pltpu
from jax.sharding import PartitionSpec as P

BLK = 32
HEAD = 128
LOG2E = 1.4426950408889634
F32 = jnp.float32
BF16 = jnp.bfloat16


def nt(a, b):
    return lax.dot_general(a, b, (((1,), (1,)), ((), ())), preferred_element_type=F32)


def nn(a, b):
    return jnp.dot(a, b, preferred_element_type=F32)


def kernel(
    planes, groups, pairs,
    place_ref, doc_ref, own_ref, q_hbm, k_ref, v_ref, do_hbm,
    out_ref, dq_ref, dk_ref, dv_ref,
    kvb, part, half, zbuf, lastb, s_buf, e_buf, kt, vt, acc, sums, bias_ref, q_ref, do_ref, load_sem,
    ag_send, ag_recv, rs_send, rs_recv,
):
    loads = (
        pltpu.make_async_copy(q_hbm, q_ref, load_sem.at[0]),
        pltpu.make_async_copy(do_hbm, do_ref, load_sem.at[1]),
    )
    for load in loads:
        load.start()
    rows = q_ref.shape[0]
    tile = 4 * rows
    scale = HEAD ** (-0.5)
    me = lax.axis_index("ctx")
    x = lax.rem(me, 2)
    y = lax.rem(me // 2, 2)
    z = me // 4
    peer_x = me + 1 - 2 * x
    peer_y = me + 2 - 4 * y
    top = planes - 1

    def remote(src, dst, send, recv, device):
        return pltpu.make_async_remote_copy(
            src_ref=src, dst_ref=dst, send_sem=send, recv_sem=recv,
            device_id={"ctx": device}, device_id_type=pl.DeviceIdType.MESH,
        )

    def ag_copy(g, v, index, ref, device):
        return remote(ref, ref, ag_send.at[g, v, index], ag_recv.at[g, v, index], device)

    def pair_of(g, v, plane):
        return kvb.at[g, 0, plane, y] if v == 0 else kvb.at[g, 1, plane, :, x]

    def ag_first(g, v):
        return ag_copy(g, v, 0, kvb.at[g, v, z, y, x], peer_x if v == 0 else peer_y)

    def ag_first_in(g, v):
        ref = kvb.at[g, 0, z, y, 1 - x] if v == 0 else kvb.at[g, 1, z, 1 - y, x]
        return ag_copy(g, v, 0, ref, peer_x if v == 0 else peer_y)

    def ag_up(g, v, j, plane):
        return ag_copy(g, v, 1 + j, pair_of(g, v, plane), me + 4)

    def ag_down(g, v, j, plane):
        return ag_copy(g, v, planes + j, pair_of(g, v, plane), me - 4)

    def ag_last(g, v, plane):
        return ag_copy(g, v, 2 * planes - 1 + plane, pair_of(g, v, plane), peer_y if v == 0 else peer_x)

    def ag_last_in(g, v, plane):
        ref = kvb.at[g, 0, plane, 1 - y] if v == 0 else kvb.at[g, 1, plane, :, 1 - x]
        return ag_copy(g, v, 2 * planes - 1 + plane, ref, peer_y if v == 0 else peer_x)

    def one_up(g, v, j, plane):
        return ag_copy(g, v, 1 + j, kvb.at[g, v, plane, y, x], me + 4)

    def one_down(g, v, j, plane):
        return ag_copy(g, v, planes + j, kvb.at[g, v, plane, y, x], me - 4)

    def one_side(g, v, plane):
        return ag_copy(g, v, 3 * planes - 1 + plane, kvb.at[g, v, plane, y, x],
                       peer_x if v == 0 else peer_y)

    def one_side_in(g, v, plane):
        ref = kvb.at[g, 0, plane, y, 1 - x] if v == 0 else kvb.at[g, 1, plane, 1 - y, x]
        return ag_copy(g, v, 3 * planes - 1 + plane, ref, peer_x if v == 0 else peer_y)

    def ag_step_z(k, g):
        for v in range(2):
            if k == 0:
                @pl.when(z < top)
                def _():
                    one_up(g, v, 0, z).start()

                @pl.when(z > 0)
                def _():
                    one_down(g, v, 0, z).start()

                one_side(g, v, z).start()
            elif k <= planes:
                if k < planes:
                    @pl.when(z >= k)
                    def _():
                        one_up(g, v, k - 1, z - k).wait_recv()
                        if k < top:
                            @pl.when(z < top)
                            def _():
                                one_up(g, v, k, z - k).start()
                        one_side(g, v, z - k).start()

                    @pl.when(z + k <= top)
                    def _():
                        one_down(g, v, k - 1, z + k).wait_recv()
                        if k < top:
                            @pl.when(z > 0)
                            def _():
                                one_down(g, v, k, z + k).start()
                        one_side(g, v, z + k).start()
                j = k - 1
                if j == 0:
                    one_side_in(g, v, z).wait_recv()
                    ag_last(g, v, z).start()
                else:
                    @pl.when(z >= j)
                    def _():
                        one_side_in(g, v, z - j).wait_recv()
                        ag_last(g, v, z - j).start()

                    @pl.when(z + j <= top)
                    def _():
                        one_side_in(g, v, z + j).wait_recv()
                        ag_last(g, v, z + j).start()
            else:
                for plane in range(planes):
                    ag_last_in(g, v, plane).wait_recv()
                    ag_last(g, v, plane).wait_send()
                    one_side(g, v, plane).wait_send()
                for j in range(top):
                    @pl.when(jnp.logical_and(z < top, z >= j))
                    def _():
                        one_up(g, v, j, z - j).wait_send()

                    @pl.when(jnp.logical_and(z > 0, z + j <= top))
                    def _():
                        one_down(g, v, j, z + j).wait_send()

    def ag_step(k, g):
        if g % 2 == 1:
            ag_step_z(k, g)
            return
        for v in range(2):
            if k == 0:
                ag_first(g, v).start()
            elif k == 1:
                ag_first_in(g, v).wait_recv()

                @pl.when(z < top)
                def _():
                    ag_up(g, v, 0, z).start()

                @pl.when(z > 0)
                def _():
                    ag_down(g, v, 0, z).start()

                ag_last(g, v, z).start()
            elif k <= planes:
                j = k - 1

                @pl.when(z >= j)
                def _():
                    ag_up(g, v, j - 1, z - j).wait_recv()
                    if j < top:
                        @pl.when(z < top)
                        def _():
                            ag_up(g, v, j, z - j).start()
                    ag_last(g, v, z - j).start()

                @pl.when(z + j <= top)
                def _():
                    ag_down(g, v, j - 1, z + j).wait_recv()
                    if j < top:
                        @pl.when(z > 0)
                        def _():
                            ag_down(g, v, j, z + j).start()
                    ag_last(g, v, z + j).start()
            else:
                for plane in range(planes):
                    ag_last_in(g, v, plane).wait_recv()
                    ag_last(g, v, plane).wait_send()
                ag_first(g, v).wait_send()
                for j in range(top):
                    @pl.when(jnp.logical_and(z < top, z >= j))
                    def _():
                        ag_up(g, v, j, z - j).wait_send()

                    @pl.when(jnp.logical_and(z > 0, z + j <= top))
                    def _():
                        ag_down(g, v, j, z + j).wait_send()

    def rs_half(g, v, t):
        src = part.at[g, 0, t, 1 - y] if v == 0 else part.at[g, 1, t, :, 1 - x]
        index = 2 * planes + 1 + t
        return remote(src, half.at[g, v, t], rs_send.at[g, v, index], rs_recv.at[g, v, index],
                      peer_y if v == 0 else peer_x)

    def rs_flow(g, v, way, t):
        index = way * planes + t
        return remote(half.at[g, v, t], zbuf.at[g, v, way, t], rs_send.at[g, v, index],
                      rs_recv.at[g, v, index], me + 4 - 8 * way)

    def rs_last(g, v):
        index = 2 * planes
        src = half.at[g, 0, z, 1 - x] if v == 0 else half.at[g, 1, z, 1 - y]
        return remote(src, lastb.at[g, v], rs_send.at[g, v, index], rs_recv.at[g, v, index],
                      peer_x if v == 0 else peer_y)

    def joined(g, v, t):
        own = part[g, 0, t, y] if v == 0 else part[g, 1, t, :, x]
        return half[g, v, t].astype(F32) + own.astype(F32)

    def rs_step(k, g):
        if k == 0:
            for i in range(planes):
                for v in range(2):
                    @pl.when(top - i > z)
                    def _():
                        rs_half(g, v, top - i).start()

                    @pl.when(i < z)
                    def _():
                        rs_half(g, v, i).start()
            for v in range(2):
                rs_half(g, v, z).start()
            return
        for v in range(2):
            if k < planes:
                s = k - 1
                for way in range(2):
                    place = z if way == 0 else top - z
                    dist = top - (s - place)
                    t = dist if way == 0 else top - dist

                    @pl.when(jnp.logical_and(s >= place, dist > place))
                    def _():
                        rs_half(g, v, t).wait_recv()

                        @pl.when(place == 0)
                        def _():
                            half[g, v, t] = joined(g, v, t).astype(BF16)

                        @pl.when(place > 0)
                        def _():
                            rs_flow(g, v, way, t).wait_recv()
                            half[g, v, t] = (joined(g, v, t) + zbuf[g, v, way, t].astype(F32)).astype(BF16)

                        rs_flow(g, v, way, t).start()
            elif k == planes:
                rs_half(g, v, z).wait_recv()
                sums[...] = joined(g, v, z)

                @pl.when(z > 0)
                def _():
                    rs_flow(g, v, 0, z).wait_recv()
                    sums[...] += zbuf[g, v, 0, z].astype(F32)

                @pl.when(z < top)
                def _():
                    rs_flow(g, v, 1, z).wait_recv()
                    sums[...] += zbuf[g, v, 1, z].astype(F32)

                half[g, v, z] = sums[...].astype(BF16)
                rs_last(g, v).start()
            else:
                rs_last(g, v).wait_recv()
                own = half[g, 0, z, x] if v == 0 else half[g, 1, z, y]
                total = (own.astype(F32) + lastb[g, v].astype(F32)).astype(BF16)
                cols = pl.ds(pl.multiple_of(g * HEAD, HEAD), HEAD)
                (dk_ref if v == 0 else dv_ref)[:, cols] = total
                rs_last(g, v).wait_send()
                for t in range(planes):
                    rs_half(g, v, t).wait_send()

                    @pl.when(t > z)
                    def _():
                        rs_flow(g, v, 0, t).wait_send()

                    @pl.when(t < z)
                    def _():
                        rs_flow(g, v, 1, t).wait_send()

    steps = planes + 2

    barrier = pltpu.get_barrier_semaphore()
    for peer in (peer_x, peer_y):
        pl.semaphore_signal(barrier, inc=1, device_id={"ctx": peer}, device_id_type=pl.DeviceIdType.MESH)

    @pl.when(z < top)
    def _():
        pl.semaphore_signal(barrier, inc=1, device_id={"ctx": me + 4}, device_id_type=pl.DeviceIdType.MESH)

    @pl.when(z > 0)
    def _():
        pl.semaphore_signal(barrier, inc=1, device_id={"ctx": me - 4}, device_id_type=pl.DeviceIdType.MESH)

    for g in range(groups):
        kvb[g, 0, z, y, x] = k_ref[:, g * HEAD:(g + 1) * HEAD]
        kvb[g, 1, z, y, x] = v_ref[:, g * HEAD:(g + 1) * HEAD]
    pl.semaphore_wait(barrier, 2 + (z < top).astype(jnp.int32) + (z > 0).astype(jnp.int32))

    def ag_slot(slot):
        for g in reversed(range(groups)):
            if slot == 2 * g:
                ag_step(0, g)
        for g in range(groups):
            if 0 < slot - 2 * g < steps:
                ag_step(slot - 2 * g, g)

    ag_slot(0)
    ag_slot(1)
    own_place = own_ref[0:1, :]
    own_doc = own_ref[1:2, :]
    for c in range(bias_ref.shape[0] // HEAD):
        span = slice(c * HEAD, (c + 1) * HEAD)
        place_col = jnp.broadcast_to(place_ref[:, span], (HEAD, HEAD)).T
        doc_col = jnp.broadcast_to(doc_ref[:, span], (HEAD, HEAD)).T
        allowed = jnp.logical_and(doc_col == own_doc, place_col <= own_place)
        bias_ref[span, :] = jnp.where(allowed, 0.0, -1e30)
    for slot in range(2, steps):
        ag_slot(slot)
    for load in loads:
        load.wait()

    points = 2 * pairs

    def beside(place, g, p):
        here = g * points + 2 * p + place
        for i in range(2 * (groups - 1)):
            if (1 + 2 * i) % 2 == place:
                @pl.when(here == 1 + 2 * i)
                def _():
                    ag_slot(steps + i)
        for k in range(steps):
            point = min(k if k == 0 else k + 1, points - 1)
            if point % 2 == place:
                @pl.when(jnp.logical_and(p == point // 2, g > 0))
                def _():
                    rs_step(k, g - 1)

    def keys(g, v, t):
        return kvb[g, v, t].reshape(tile, HEAD)

    def head(g, carry):
        for t in range(planes):
            kt[:, t * tile:(t + 1) * tile] = keys(g, 0, t).T
            vt[:, t * tile:(t + 1) * tile] = keys(g, 1, t).T
        acc[...] = jnp.zeros_like(acc)

        def pair(p, carry):
            start = pl.multiple_of((g * pairs + p) * 2 * HEAD, HEAD)
            col0 = pl.ds(start, HEAD)
            col1 = pl.ds(pl.multiple_of(start + HEAD, HEAD), HEAD)
            q2 = jnp.concatenate([q_ref[:, col0], q_ref[:, col1]], axis=0)
            wide = q2.shape[0]
            most = jnp.full((8, wide), -jnp.inf, F32)
            for t in range(planes):
                b = bias_ref[t * tile:(t + 1) * tile, :]
                s = nt(keys(g, 0, t), q2) + jnp.concatenate([b, b], axis=1)
                s_buf[t * tile:(t + 1) * tile, :] = s
                most = jnp.maximum(most, jnp.max(s.reshape(tile // 8, 8, wide), axis=0))
            beside(0, g, p)
            lift = jnp.max(most, axis=0, keepdims=True) * (scale * LOG2E)
            total = jnp.zeros((8, wide), F32)
            o_t = jnp.zeros((HEAD, wide), F32)
            for t in range(planes):
                e = jnp.exp2(s_buf[t * tile:(t + 1) * tile, :] * (scale * LOG2E) - lift)
                total = total + jnp.sum(e.reshape(tile // 8, 8, wide), axis=0)
                eb = e.astype(BF16)
                e_buf[t * tile:(t + 1) * tile, :] = eb
                o_t = o_t + nn(vt[:, t * tile:(t + 1) * tile], eb)
            inv = 1.0 / jnp.sum(total, axis=0, keepdims=True)
            o_t = (o_t * inv).astype(BF16).astype(F32)
            o2 = o_t.T.astype(BF16)
            out_ref[:, col0] = o2[:rows]
            out_ref[:, col1] = o2[rows:]
            do2 = jnp.concatenate([do_ref[:, col0], do_ref[:, col1]], axis=0).astype(F32)
            delta = jnp.sum(do2.T * o_t, axis=0, keepdims=True) * inv
            dos = (do2 * jnp.broadcast_to(inv, (HEAD, wide)).T).astype(BF16)
            dq_t = jnp.zeros((HEAD, wide), F32)
            for t in range(planes):
                span = slice(t * tile, (t + 1) * tile)
                dp = nt(keys(g, 1, t), dos)
                eb = e_buf[span, :]
                ds = (eb.astype(F32) * (dp - delta)).astype(BF16)
                acc[0, span, :] += nn(ds, q2)
                acc[1, span, :] += nn(eb, dos)
                dq_t = dq_t + nn(kt[:, span], ds)
            dq2 = (dq_t * scale).T.astype(BF16)
            dq_ref[:, col0] = dq2[:rows]
            dq_ref[:, col1] = dq2[rows:]
            beside(1, g, p)
            return carry

        lax.fori_loop(0, pairs, pair, 0)
        for t in range(planes):
            span = slice(t * tile, (t + 1) * tile)
            part[g, 0, t] = (acc[0, span, :] * scale).astype(BF16).reshape(2, 2, rows, HEAD)
            part[g, 1, t] = acc[1, span, :].astype(BF16).reshape(2, 2, rows, HEAD)
        return carry

    lax.fori_loop(0, groups, head, 0)
    for k in range(steps):
        rs_step(k, groups - 1)


def body(doc_lengths, assignment, queries, key_state_rows, value_state_rows, out_grad):
    rows = queries.shape[0]
    blocks = assignment.shape[0]
    total = blocks * BLK
    devices = total // rows
    planes = devices // 4
    groups = key_state_rows.shape[1] // HEAD
    pairs = queries.shape[1] // key_state_rows.shape[1] // 2
    bounds = jnp.cumsum(doc_lengths)
    per = rows // BLK
    own = lax.dynamic_slice_in_dim(assignment, lax.axis_index("ctx") * per, per)
    offset = jnp.arange(BLK, dtype=jnp.int32)
    key_place = (assignment[:, None] * BLK + offset[None, :]).reshape(-1)
    query_place = (own[:, None] * BLK + offset[None, :]).reshape(-1)
    key_doc = jnp.sum((bounds[None, :] <= key_place[:, None]).astype(jnp.int32), axis=1)
    query_doc = jnp.sum((bounds[None, :] <= query_place[:, None]).astype(jnp.int32), axis=1)
    places = key_place.astype(F32)[None, :]
    docs = key_doc.astype(F32)[None, :]
    mine = jnp.stack([query_place, query_doc]).astype(F32)

    ag_sems = 4 * planes - 1
    rs_sems = 3 * planes + 1
    vmem = pl.BlockSpec(memory_space=pltpu.VMEM)
    hbm = pl.BlockSpec(memory_space=pl.ANY)
    return pl.pallas_call(
        functools.partial(kernel, planes, groups, pairs),
        out_shape=(
            jax.ShapeDtypeStruct(queries.shape, BF16),
            jax.ShapeDtypeStruct(queries.shape, BF16),
            jax.ShapeDtypeStruct(key_state_rows.shape, BF16),
            jax.ShapeDtypeStruct(key_state_rows.shape, BF16),
        ),
        in_specs=[vmem, vmem, vmem, hbm, vmem, vmem, hbm],
        out_specs=(vmem,) * 4,
        scratch_shapes=[
            pltpu.VMEM((groups, 2, planes, 2, 2, rows, HEAD), BF16),
            pltpu.VMEM((groups, 2, planes, 2, 2, rows, HEAD), BF16),
            pltpu.VMEM((groups, 2, planes, 2, rows, HEAD), BF16),
            pltpu.VMEM((groups, 2, 2, planes, 2, rows, HEAD), BF16),
            pltpu.VMEM((groups, 2, rows, HEAD), BF16),
            pltpu.VMEM((total, 2 * rows), F32),
            pltpu.VMEM((total, 2 * rows), BF16),
            pltpu.VMEM((HEAD, total), BF16),
            pltpu.VMEM((HEAD, total), BF16),
            pltpu.VMEM((2, total, HEAD), F32),
            pltpu.VMEM((2, rows, HEAD), F32),
            pltpu.VMEM((total, rows), F32),
            pltpu.VMEM(queries.shape, BF16),
            pltpu.VMEM(queries.shape, BF16),
            pltpu.SemaphoreType.DMA((2,)),
            pltpu.SemaphoreType.DMA((groups, 2, ag_sems)),
            pltpu.SemaphoreType.DMA((groups, 2, ag_sems)),
            pltpu.SemaphoreType.DMA((groups, 2, rs_sems)),
            pltpu.SemaphoreType.DMA((groups, 2, rs_sems)),
        ],
        compiler_params=pltpu.CompilerParams(
            collective_id=0, has_side_effects=True, vmem_limit_bytes=58 * 1024 * 1024
        ),
        cost_estimate=pl.CostEstimate(
            flops=12 * queries.shape[0] * queries.shape[1] * total,
            bytes_accessed=8 * queries.size,
            transcendentals=queries.shape[0] * queries.shape[1] // HEAD * total,
        ),
    )(places, docs, mine, queries, key_state_rows, value_state_rows, out_grad)


def solution(mesh):
    row = P(("dp", "ctx"), None)
    return jax.shard_map(
        body,
        mesh=mesh,
        in_specs=(P("dp"), P("dp"), row, row, row, row),
        out_specs=(row, row, row, row),
        check_vma=False,
    )
```
